32 devices in a mesh: grp: 2 (over y), lon: 4 (over z), ch: 4 (over x, core).
Axes of the slice: x: 2, y: 2, z: 4, core: 2. Of those that a mesh axis runs over, the one named last changes fastest.
Arguments:
- field_in: bfloat16 [512, 64, 128], P('ch', ('grp', 'lon')), parts along dimension 1
- sea_mask: int32 [32, 128], P('lon'), may hold values 0 or 1
- fold_partner: int32 [4], replicated, may hold values from 0 to 3, as said below
- kernel: float32 [512, 7, 7], P('ch'), may hold values from -0.875 to 0.875
- ln_gain: float32 [512], replicated, may hold values from 0.5 to 1.5
- ln_shift: float32 [512], replicated, may hold values from -3 to 3
- w_in: bfloat16 [512, 1024], P(None, 'ch'), may hold values from -0.25 to 0.25
- w_out: bfloat16 [1024, 512], P('ch'), may hold values from -0.1875 to 0.1875
- layer_scale: float32 [512], P('ch'), may hold values from 0.25 to 1.75
- grad_out: bfloat16 [512, 64, 128], P('ch', ('grp', 'lon')), parts along dimension 1, may hold values from -6 to 6
Outputs:
- block_out: bfloat16 [512, 64, 128], P('ch', ('grp', 'lon')), parts along dimension 1
- grad_x: bfloat16 [512, 64, 128], P('ch', ('grp', 'lon')), parts along dimension 1
- grad_kernel: float32 [1024, 7, 7], P(('grp', 'ch')), parts along dimension 0
- grad_w_in: float32 [1024, 1024], P('grp', 'ch'), parts along dimension 0
- grad_w_out: float32 [2048, 512], P(('grp', 'ch')), parts along dimension 0
The draws below stay inside these ranges and needn't reach their ends.
There are 2 independent parts, one for each index of `grp`. The reference program is written for one: setup_inputs(seed, part) draws one part's arguments, and reference() takes and returns one part's arrays. A program takes and returns all parts, laid end to end along the dimension named above; an argument that names none is the same for every part. Nothing has to cross between parts.
Inputs may be any that keep to these rules, and one draw needn't show every extreme that they name: fold_partner[fold_partner[t]] = t for every tile t; a tile may face itself, and at least one tile faces another tile.
All inputs are finite; a program needn't handle non-finite values. No bound on the sum of `sea_mask` on one device may be relied on, other than what follows from the above.
Results may differ from the reference program's by a relative error of at most 0.0063.
Values may be sent and summed in bfloat16 or wider, within the bound.
A program may use at most 64 MiB of HBM per device.

```python
import math
import jax
import jax.numpy as jnp
from jax import lax

D = 512
FF = 1024
LAT = 128
LON_DEV = 8
TILES = 4
LON = 32


def draw_field_in(key, part):
    key_one, key_two = jax.random.split(key, 2)
    lon_all = LON_DEV * TILES
    position = jnp.arange(D, dtype=jnp.float32) / D
    spread = jnp.exp(jax.random.uniform(key_one, (D,), jnp.float32, 0.0, math.log(10.0)))
    chan_scale = 0.2 * spread * jnp.exp(position * math.log(3.0))
    values = jax.random.normal(key_two, (D, lon_all, LAT), jnp.float32) * chan_scale[:, None, None]
    return values.astype(jnp.bfloat16)


def draw_fold_partner(key, part):
    key_pairs, key_coins = jax.random.split(jax.random.fold_in(key, 7919), 2)
    shuffled = jax.random.permutation(key_pairs, TILES).astype(jnp.int32)
    tile_pairs = shuffled.reshape(TILES // 2, 2)
    coins = jax.random.randint(key_coins, (TILES // 2,), 0, 2).astype(jnp.int32)
    coins = coins.at[0].set(1)
    first_target = jnp.where(coins == 1, tile_pairs[:, 1], tile_pairs[:, 0]).astype(jnp.int32)
    second_target = jnp.where(coins == 1, tile_pairs[:, 0], tile_pairs[:, 1]).astype(jnp.int32)
    partner = jnp.zeros((TILES,), jnp.int32)
    partner = partner.at[tile_pairs[:, 0]].set(first_target)
    partner = partner.at[tile_pairs[:, 1]].set(second_target)
    return partner


def with_ends(entries, rng, smallest, largest):
    index_at = [jax.random.randint(jax.random.fold_in(rng, axis), (), 0, length) for axis, length in enumerate(entries.shape)]
    widest = entries.shape.index(max(entries.shape))
    beside = index_at[:widest] + [(index_at[widest] + 1) % entries.shape[widest]] + index_at[widest + 1:]
    return entries.at[tuple(index_at)].set(smallest).at[tuple(beside)].set(largest)


def levels(own_key, shape, pieces, least, top_value):
    factor_of, own = 1.0, jax.random.fold_in(own_key, 6)
    for dim, shards_of in pieces:
        draws = jnp.exp(jax.random.uniform(jax.random.fold_in(own, dim), (shards_of,), jnp.float32, least / len(pieces), top_value / len(pieces)))
        factor_of = factor_of * jnp.repeat(draws, shape[dim] // shards_of).reshape([-1 if axis == dim else 1 for axis in range(len(shape))])
    return factor_of


def bell_draw(own_key, extent, width, reach, pieces=(), kind=jnp.bfloat16):
    level = levels(own_key, extent, pieces, -0.22, 0.18) if pieces else 1.0
    result = jax.random.normal(own_key, extent, jnp.float32) * width * level
    return jnp.minimum(jnp.maximum(result, -reach), reach).astype(kind)


def setup_inputs(seed: int = 0, part: int = 0) -> dict:
    seeds = jax.random.split(jax.random.key(seed), 11)
    own_keys = jax.random.split(jax.random.fold_in(seeds[10], part), 11)
    return {
        "field_in": draw_field_in(jax.random.fold_in(jax.random.fold_in(seeds[10], part), 71), part),
        "sea_mask": with_ends((jax.random.randint(seeds[1], (LON, LAT), 0, 4) < 3).astype(jnp.int32), jax.random.fold_in(seeds[1], 1), 0, 1),
        "fold_partner": draw_fold_partner(jax.random.fold_in(seeds[10], 71), part),
        "kernel": bell_draw(seeds[3], (D, 7, 7), 49 ** -0.5, 0.875, ((0, 4),), jnp.float32),
        "ln_gain": jnp.clip(1.0 + 0.1 * jax.random.normal(seeds[4], (D,), jnp.float32), 0.5, 1.5),
        "ln_shift": bell_draw(seeds[5], (D,), 0.5, 3.0, (), jnp.float32),
        "w_in": bell_draw(seeds[6], (D, FF), D ** -0.5, 0.25, ((1, 4),)),
        "w_out": bell_draw(seeds[7], (FF, D), FF ** -0.5, 0.1875, ((0, 4),)),
        "layer_scale": jnp.clip(1.0 + 0.15 * jax.random.normal(seeds[8], (D,), jnp.float32), 0.25, 1.75),
        "grad_out": bell_draw(own_keys[9], (D, LON, LAT), 1.0, 6.0, ((0, 4), (1, 4))),
    }


EPSILON = 1e-06

def gelu_parts(hidden):
    normal_cdf = 0.5 * (1.0 + jax.scipy.special.erf(hidden * (1.0 / math.sqrt(2.0))))
    density = jnp.exp(-0.5 * hidden * hidden) * (1.0 / math.sqrt(2.0 * math.pi))
    return (hidden * normal_cdf, normal_cdf + hidden * density)

def reference(field_in, sea_mask, fold_partner, kernel, ln_gain, ln_shift, w_in, w_out, layer_scale, grad_out):
    lon_all = LON_DEV * TILES
    cell_count = lon_all * LAT
    ocean_f = sea_mask.astype(jnp.float32)[None]
    masked = field_in * sea_mask.astype(jnp.bfloat16)[None]
    column_ids = jnp.arange(lon_all, dtype=jnp.int32)
    mirror = (fold_partner[column_ids // LON_DEV] * LON_DEV + (LON_DEV - 1 - column_ids % LON_DEV)).astype(jnp.int32)
    top_rows = masked[:, :, LAT - 3:][:, :, ::-1]
    fold_rows = jnp.take(top_rows, mirror, axis=1)
    south_rows = jnp.zeros((D, lon_all, 3), jnp.bfloat16)
    tall_field = jnp.concatenate([south_rows, masked, fold_rows], axis=2)
    extended = jnp.concatenate([tall_field[:, lon_all - 3:], tall_field, tall_field[:, :3]], axis=1).astype(jnp.float32)
    mix_field = jnp.zeros((D, lon_all, LAT), jnp.float32)
    for row_tap in range(7):
        for col_tap in range(7):
            mix_field = mix_field + kernel[:, row_tap, col_tap][:, None, None] * extended[:, row_tap:row_tap + lon_all, col_tap:col_tap + LAT]
    mean_cell = lax.optimization_barrier(jnp.sum(mix_field, axis=0)) / D
    inv_sigma = lax.rsqrt(lax.optimization_barrier(jnp.sum(mix_field * mix_field, axis=0)) / D - mean_cell * mean_cell + EPSILON)
    centred = (mix_field - mean_cell) * inv_sigma
    normed = (centred * ln_gain[:, None, None] + ln_shift[:, None, None]).astype(jnp.bfloat16).reshape(D, cell_count)
    hidden = jnp.dot(normed.T, w_in, preferred_element_type=jnp.float32)
    activation, gelu_slope = gelu_parts(hidden)
    activated = activation.astype(jnp.bfloat16)
    branch = jnp.dot(w_out.T, activated.T, preferred_element_type=jnp.float32)
    grad_f = grad_out.astype(jnp.float32)
    block_out = (ocean_f * (field_in.astype(jnp.float32) + layer_scale[:, None, None] * branch.reshape(D, lon_all, LAT))).astype(jnp.bfloat16)
    scaled_grad = (ocean_f * layer_scale[:, None, None] * grad_f).astype(jnp.bfloat16).reshape(D, cell_count)
    activated_grad = jnp.dot(scaled_grad.T, w_out.T, preferred_element_type=jnp.float32)
    raw_w_out = jnp.dot(activated.T, scaled_grad.T, preferred_element_type=jnp.float32)
    hidden_grad = (activated_grad * gelu_slope).astype(jnp.bfloat16)
    raw_w_in = jnp.dot(normed, hidden_grad, preferred_element_type=jnp.float32)
    normed_grad = jnp.dot(w_in, hidden_grad.T, preferred_element_type=jnp.float32)
    scaled_normed = normed_grad.reshape(D, lon_all, LAT) * ln_gain[:, None, None]
    mixed_grad = inv_sigma * (scaled_normed - lax.optimization_barrier(jnp.sum(scaled_normed, axis=0)) / D - centred * (lax.optimization_barrier(jnp.sum(scaled_normed * centred, axis=0)) / D))
    tap_sums = []
    for row_tap in range(7):
        for col_tap in range(7):
            tap_sums.append(lax.optimization_barrier(jnp.sum(extended[:, row_tap:row_tap + lon_all, col_tap:col_tap + LAT] * mixed_grad, axis=(1, 2))))
    raw_kernel = jnp.stack(tap_sums, axis=1).reshape(D, 7, 7)
    padded = jnp.pad(mixed_grad, ((0, 0), (6, 6), (6, 6)))
    extended_grad = jnp.zeros((D, lon_all + 6, LAT + 6), jnp.float32)
    for row_tap in range(7):
        for col_tap in range(7):
            extended_grad = extended_grad + kernel[:, row_tap, col_tap][:, None, None] * padded[:, 6 - row_tap:6 - row_tap + lon_all + 6, 6 - col_tap:6 - col_tap + LAT + 6]
    tall_grad = extended_grad[:, 3:3 + lon_all]
    tall_grad = tall_grad.at[:, lon_all - 3:].add(extended_grad[:, :3])
    tall_grad = tall_grad.at[:, :3].add(extended_grad[:, lon_all + 3:])
    fold_grad = tall_grad[:, :, 3 + LAT:]
    fold_back = jnp.take(fold_grad, mirror, axis=1)[:, :, ::-1]
    field_grad = tall_grad[:, :, 3:3 + LAT].at[:, :, LAT - 3:].add(fold_back)
    grad_x = (ocean_f * (grad_f + field_grad)).astype(jnp.bfloat16)
    factor = 1.0 / math.sqrt(cell_count)
    return (block_out, grad_x, raw_kernel * factor, raw_w_in * factor, raw_w_out * factor)
```

```python
import functools
import math

import jax
import jax.numpy as jnp
from jax import lax
from jax.experimental import pallas as pl
from jax.experimental.pallas import tpu as pltpu
from jax.sharding import PartitionSpec as P

EPSILON = 1e-06
F32 = jnp.float32
BF16 = jnp.bfloat16
MESH = pl.DeviceIdType.MESH
VMEM_SPEC = pl.BlockSpec(memory_space=pltpu.VMEM)
SMEM_SPEC = pl.BlockSpec(memory_space=pltpu.SMEM)
LIMIT = 48 * 1024 * 1024


def greet(axes):
    barrier = pltpu.get_barrier_semaphore()
    total = 0
    for axis in axes:
        count = lax.axis_size(axis)
        me = lax.axis_index(axis)
        for d in range(1, count):
            pl.semaphore_signal(
                barrier, inc=1, device_id={axis: lax.rem(me + d, count)}, device_id_type=MESH
            )
        total += count - 1
    pl.semaphore_wait(barrier, total)


def push(src, dst, sems, slot, axis, target):
    copy = pltpu.make_async_remote_copy(
        src_ref=src,
        dst_ref=dst,
        send_sem=sems[0].at[slot],
        recv_sem=sems[1].at[slot],
        device_id={axis: target},
        device_id_type=MESH,
    )
    copy.start()
    return copy


def edge_kernel(tiles, with_extra, *refs):
    if with_extra:
        x_ref, extra_ref, west_ref, east_ref, tops_ref, extras_ref, send, recv = refs
    else:
        x_ref, west_ref, east_ref, tops_ref, send, recv = refs
    me = lax.axis_index("lon")
    cols, rows = x_ref.shape[0], x_ref.shape[1]
    sems = (send, recv)
    greet(("lon",))
    right, left = lax.rem(me + 1, tiles), lax.rem(me + tiles - 1, tiles)
    copies = [
        push(x_ref.at[pl.ds(cols - 3, 3)], west_ref, sems, 0, "lon", right),
        push(x_ref.at[pl.ds(0, 3)], east_ref, sems, 1, "lon", left),
    ]
    for d in range(1, tiles):
        t = lax.rem(me + d, tiles)
        copies.append(
            push(x_ref.at[:, pl.ds(rows - 16, 16)], tops_ref.at[me], sems, 1 + d, "lon", t)
        )
        if with_extra:
            copies.append(push(extra_ref, extras_ref.at[me], sems, tiles + d, "lon", t))
    tops_ref[me] = x_ref[:, rows - 16 :]
    if with_extra:
        extras_ref[me] = extra_ref[...]
    for copy in copies:
        copy.wait()


def edges(x, extra, collective_id):
    cols, rows, chans = x.shape
    tiles = lax.axis_size("lon")
    out = [
        jax.ShapeDtypeStruct((3, rows, chans), BF16),
        jax.ShapeDtypeStruct((3, rows, chans), BF16),
        jax.ShapeDtypeStruct((tiles, cols, 16, chans), BF16),
    ]
    args = [x]
    if extra is not None:
        out.append(jax.ShapeDtypeStruct((tiles,) + extra.shape, F32))
        args.append(extra)
    return pl.pallas_call(
        functools.partial(edge_kernel, tiles, extra is not None),
        out_shape=out,
        in_specs=[VMEM_SPEC] * len(args),
        out_specs=[VMEM_SPEC] * len(out),
        scratch_shapes=[
            pltpu.SemaphoreType.DMA((2 * tiles + 1,)),
            pltpu.SemaphoreType.DMA((2 * tiles + 1,)),
        ],
        compiler_params=pltpu.CompilerParams(
            collective_id=collective_id, has_side_effects=True, vmem_limit_bytes=LIMIT
        ),
    )(*args)


def fill_shifts(ext_ref, shifts_ref, rows):
    def one(q, _):
        for b in range(7):
            shifts_ref[b, q] = ext_ref[q, pl.ds(5 + b, rows)]
        return 0

    lax.fori_loop(0, ext_ref.shape[0], one, 0)


def conv_kernel(tiles, mine_ref, partner_ref, x_ref, west_ref, east_ref, tops_ref, tap_ref,
                mix_ref, ext_ref, shifts_ref):
    cols, rows, chans = x_ref.shape
    me = mine_ref[0]
    ext_ref[...] = jnp.zeros_like(ext_ref)
    for q in range(cols + 6):
        if q < 3:
            main = west_ref[q]
        elif q < cols + 3:
            main = x_ref[q - 3]
        else:
            main = east_ref[q - cols - 3]
        ext_ref[q, pl.ds(8, rows)] = main.astype(F32)
        step, col = (q - 3) // cols, (q - 3) % cols
        tile = lax.rem(me + step + tiles, tiles)
        top = tops_ref[partner_ref[tile], cols - 1 - col].astype(F32)
        for k in range(3):
            ext_ref[q, pl.ds(8 + rows + k, 1)] = top[15 - k : 16 - k]
    fill_shifts(ext_ref, shifts_ref, rows)

    def one(i, _):
        acc = jnp.zeros((rows, chans), F32)
        for a in range(7):
            for b in range(7):
                acc = acc + tap_ref[pl.ds(a * 7 + b, 1)] * shifts_ref[b, i + a]
        mix_ref[i] = acc
        return 0

    lax.fori_loop(0, cols, one, 0)


def tap_grad_kernel(ext_ref, mg_ref, out_ref, half_ref, shifts_ref, sums_ref):
    cols, rows, chans = mg_ref.shape
    fill_shifts(ext_ref, shifts_ref, rows)
    sums_ref[...] = jnp.zeros_like(sums_ref)
    out_ref[...] = jnp.zeros_like(out_ref)

    def one(i, _):
        mg = mg_ref[i]
        half_ref[i] = mg.astype(BF16)
        for a in range(7):
            for b in range(7):
                prod = shifts_ref[b, i + a] * mg
                sums_ref[a * 7 + b] += jnp.sum(prod.reshape(rows // 8, 8, chans), axis=0)
        return 0

    lax.fori_loop(0, cols, one, 0)
    for t in range(49):
        out_ref[pl.ds(t, 1)] = jnp.sum(sums_ref[t], axis=0, keepdims=True)


def spread_kernel(tiles, mine_ref, partner_ref, mg_ref, west_ref, east_ref, tops_ref, tap_ref,
                  extras_ref, out_ref, kernel_ref, ext_ref, shifts_ref, fold_ref):
    cols, rows, chans = mg_ref.shape
    me = mine_ref[0]
    facing = partner_ref[me]
    ext_ref[...] = jnp.zeros_like(ext_ref)
    fold_ref[...] = jnp.zeros_like(fold_ref)
    for q in range(cols + 6):
        if q < 3:
            main = west_ref[q].astype(F32)
        elif q < cols + 3:
            main = mg_ref[q - 3]
        else:
            main = east_ref[q - cols - 3].astype(F32)
        ext_ref[q, pl.ds(8, rows)] = main
        step, col = (q - 3) // cols, (q - 3) % cols
        tile = lax.rem(facing + step + tiles, tiles)
        top = tops_ref[tile, col].astype(F32)
        for s in range(3):
            for k in range(3 - s):
                fold_ref[s, q, pl.ds(5 + s + k, 1)] = top[15 - k : 16 - k]
    fill_shifts(ext_ref, shifts_ref, rows)

    def one(i, _):
        acc = jnp.zeros((rows, chans), F32)
        for a in range(7):
            for b in range(7):
                acc = acc + tap_ref[pl.ds(a * 7 + b, 1)] * shifts_ref[6 - b, i + 6 - a]
        out_ref[i] = acc
        north = jnp.zeros((8, chans), F32)
        for a in range(7):
            for s in range(3):
                north = north + tap_ref[pl.ds(a * 7 + 6 - s, 1)] * fold_ref[
                    s, cols - 1 - i + 6 - a
                ]
        out_ref[i, pl.ds(rows - 8, 8)] += north
        return 0

    lax.fori_loop(0, cols, one, 0)
    kernel_ref[...] = jnp.sum(extras_ref[...], axis=0)


def gelu_parts(hidden):
    normal_cdf = 0.5 * (1.0 + lax.erf(hidden * (1.0 / math.sqrt(2.0))))
    density = jnp.exp(-0.5 * hidden * hidden) * (1.0 / math.sqrt(2.0 * math.pi))
    return (hidden * normal_cdf, normal_cdf + hidden * density)


def dot(a, b, dims):
    return lax.dot_general(a, b, (dims, ((), ())), preferred_element_type=F32)


def middle_kernel(n, tiles, factor, block,
                  mix_ref, sg_ref, win_ref, wout_ref, gain_ref, shift_ref,
                  branch_ref, mg_ref, gwin_ref, gwout_ref,
                  mixg, normed, act, agrad, hg, mean, inv, own_ng, one_acc, two_acc,
                  nsend, nrecv, bsend, brecv, psend, precv,
                  gof, gsi, gri, agi, gso, gro, ago,
                  *sem_refs):
    cells, chans = mix_ref.shape
    hid = win_ref.shape[2]
    width = n * chans
    blocks = cells // block
    m_sems, n_sems, p_sems, b_sems, i_sems, o_sems, ai_sems, ao_sems = [
        (sem_refs[2 * k], sem_refs[2 * k + 1]) for k in range(8)
    ]
    me = lax.axis_index("ch")
    lon = lax.axis_index("lon")
    greet(("ch", "lon"))
    peers = [lax.rem(me + d, n) for d in range(n)]
    spans = [lax.rem(lon + d, tiles) for d in range(tiles)]

    def loop(step):
        def one(i, _):
            step(pl.ds(pl.multiple_of(i * block, block), block))
            return 0

        lax.fori_loop(0, blocks, one, 0)

    mixg[me] = mix_ref[...].astype(BF16)
    copies = [
        push(mixg.at[me], mixg.at[me], m_sems, d, "ch", peers[d]) for d in range(1, n)
    ]

    def grads(rows):
        total = dot(sg_ref[0, rows], wout_ref[0], ((1,), (1,)))
        for j in range(1, n):
            total = total + dot(sg_ref[j, rows], wout_ref[j], ((1,), (1,)))
        agrad[rows] = total

    loop(grads)
    for copy in copies:
        copy.wait()

    def forward(rows):
        parts = [mixg[j, rows].astype(F32) for j in range(n)]
        one = functools.reduce(jnp.add, parts)
        two = functools.reduce(jnp.add, [v * v for v in parts])
        mean_cell = jnp.sum(one, axis=1, keepdims=True) / width
        sigma = lax.rsqrt(
            jnp.sum(two, axis=1, keepdims=True) / width - mean_cell * mean_cell + EPSILON
        )
        mean[rows] = mean_cell
        inv[rows] = sigma
        hidden = jnp.zeros((block, hid), F32)
        for j in range(n):
            value = ((parts[j] - mean_cell) * sigma * gain_ref[j] + shift_ref[j]).astype(BF16)
            normed[j, rows] = value
            hidden = hidden + dot(value, win_ref[j], ((1,), (0,)))
        activation, slope = gelu_parts(hidden)
        act[rows] = activation.astype(BF16)
        hg[rows] = (agrad[rows] * slope).astype(BF16)
        one_acc[rows] = jnp.zeros((block, chans), F32)
        two_acc[rows] = jnp.zeros((block, chans), F32)

    loop(forward)

    ncopies = []
    for d in list(range(1, n)) + [0]:
        t = peers[d]

        def back(rows, d=d, t=t):
            part = dot(hg[rows], win_ref[t], ((1,), (1,)))
            if d:
                nsend[d, rows] = part.astype(BF16)
            else:
                own_ng[rows] = part
            scaled = part * gain_ref[t]
            centred = (mixg[t, rows].astype(F32) - mean[rows]) * inv[rows]
            one_acc[rows] += scaled
            two_acc[rows] += scaled * centred

        loop(back)
        if d:
            ncopies.append(push(nsend.at[d], nrecv.at[d], n_sems, d, "ch", t))
    lane = lax.broadcasted_iota(jnp.int32, (cells, 128), 1)
    pair = jnp.where(
        lane == 0,
        jnp.sum(one_acc[...], axis=1, keepdims=True),
        jnp.sum(two_acc[...], axis=1, keepdims=True),
    )
    psend[...] = pair.T[:8]
    pcopies = [push(psend, precv.at[d], p_sems, d, "ch", peers[d]) for d in range(1, n)]

    for j in range(n):
        part = dot(act[...], sg_ref[j], ((0,), (0,)))
        gof[pl.ds(j * hid, hid)] = part
        gso[pl.ds(j * hid, hid)] = part.astype(BF16)
    ro, ri = n * hid // tiles, width // tiles
    rcopies = []
    for d in range(1, tiles):
        src = gso.at[pl.ds(pl.multiple_of(spans[d] * ro, ro), ro)]
        rcopies.append(push(src, gro.at[d], o_sems, d, "lon", spans[d]))
    for j in range(n):
        part = dot(normed[j], hg[...], ((0,), (0,)))
        gwin_ref[pl.ds(j * chans, chans)] = part
        gsi[pl.ds(j * chans, chans)] = part.astype(BF16)
    for d in range(1, tiles):
        src = gsi.at[pl.ds(pl.multiple_of(spans[d] * ri, ri), ri)]
        rcopies.append(push(src, gri.at[d], i_sems, d, "lon", spans[d]))

    bcopies = []
    for d in range(1, n):
        t = peers[d]

        def out(rows, d=d, t=t):
            bsend[d, rows] = dot(act[rows], wout_ref[t], ((1,), (0,))).astype(BF16)

        loop(out)
        bcopies.append(push(bsend.at[d], brecv.at[d], b_sems, d, "ch", t))

    def out_own(rows):
        branch_ref[rows] = dot(act[rows], wout_ref[me], ((1,), (0,)))

    loop(out_own)

    for copy in rcopies:
        copy.wait()
    own_o = gof[pl.ds(pl.multiple_of(lon * ro, ro), ro)]
    own_i = gwin_ref[pl.ds(pl.multiple_of(lon * ri, ri), ri)]
    for d in range(1, tiles):
        own_o = own_o + gro[d].astype(F32)
        own_i = own_i + gri[d].astype(F32)
    ago[lon] = (own_o * factor).astype(BF16)
    agi[lon] = (own_i * factor).astype(BF16)
    acopies = []
    for d in range(1, tiles):
        acopies.append(push(ago.at[lon], ago.at[lon], ao_sems, d, "lon", spans[d]))
        acopies.append(push(agi.at[lon], agi.at[lon], ai_sems, d, "lon", spans[d]))

    for copy in pcopies + ncopies:
        copy.wait()
    sums = psend[...]
    for d in range(1, n):
        sums = sums + precv[d]
    cols = jnp.concatenate([sums, jnp.zeros((120, cells), F32)], axis=0).T
    one_acc_mean = cols[:, 0:1] / width
    mean_two = cols[:, 1:2] / width
    total = own_ng[...]
    for d in range(1, n):
        total = total + nrecv[d].astype(F32)
    centred = (mix_ref[...] - mean[...]) * inv[...]
    mg_ref[...] = inv[...] * (total * gain_ref[me] - one_acc_mean - centred * mean_two)

    for copy in bcopies:
        copy.wait()
    total = branch_ref[...]
    for d in range(1, n):
        total = total + brecv[d].astype(F32)
    branch_ref[...] = total
    for copy in acopies:
        copy.wait()
    for t in range(tiles):
        gwin_ref[pl.ds(t * ri, ri)] = agi[t].astype(F32)
        for u in range(t * ro, (t + 1) * ro, min(ro, hid)):
            size = min(ro, hid)
            j, f = u // hid, u % hid
            gwout_ref[pl.ds(f, size), pl.ds(j * chans, chans)] = ago[
                t, pl.ds(u - t * ro, size)
            ].astype(F32)


def middle(mix, sg_all, win, wout, gain, shift, factor):
    cells, chans = mix.shape
    n, _, hid = win.shape
    tiles = lax.axis_size("lon")
    width = n * chans
    ro, ri = n * hid // tiles, width // tiles
    S = pltpu.VMEM
    scratch = [
        S((n, cells, chans), BF16), S((n, cells, chans), BF16),
        S((cells, hid), BF16), S((cells, hid), F32), S((cells, hid), BF16),
        S((cells, 1), F32), S((cells, 1), F32), S((cells, chans), F32),
        S((cells, chans), F32), S((cells, chans), F32),
        S((n, cells, chans), BF16), S((n, cells, chans), BF16),
        S((n, cells, chans), BF16), S((n, cells, chans), BF16),
        S((8, cells), F32), S((n, 8, cells), F32),
        S((n * hid, chans), F32),
        S((width, hid), BF16), S((tiles, ri, hid), BF16), S((tiles, ri, hid), BF16),
        S((n * hid, chans), BF16), S((tiles, ro, chans), BF16), S((tiles, ro, chans), BF16),
    ]
    for count in (n, n, n, n, tiles, tiles, tiles, tiles):
        scratch += [pltpu.SemaphoreType.DMA((count,)), pltpu.SemaphoreType.DMA((count,))]
    return pl.pallas_call(
        functools.partial(middle_kernel, n, tiles, factor, 256),
        out_shape=[
            jax.ShapeDtypeStruct((cells, chans), F32),
            jax.ShapeDtypeStruct((cells, chans), F32),
            jax.ShapeDtypeStruct((width, hid), F32),
            jax.ShapeDtypeStruct((hid, width), F32),
        ],
        in_specs=[VMEM_SPEC] * 6,
        out_specs=[VMEM_SPEC] * 4,
        scratch_shapes=scratch,
        compiler_params=pltpu.CompilerParams(
            collective_id=1, has_side_effects=True, vmem_limit_bytes=LIMIT
        ),
    )(mix, sg_all, win, wout, gain, shift)


def body(
    field_in, sea_mask, fold_partner, kernel, ln_gain, ln_shift, w_in, w_out, layer_scale, grad_out
):
    chans, cols, rows = field_in.shape
    tiles = lax.axis_size("lon")
    n = lax.axis_size("ch")
    cells = cols * rows
    hid = w_in.shape[1]
    mine = lax.axis_index("lon").astype(jnp.int32).reshape(1)
    factor = 1.0 / math.sqrt(tiles * cells)
    plain = pltpu.CompilerParams(vmem_limit_bytes=LIMIT)

    ocean_f = sea_mask.astype(F32)[None]
    masked = (field_in * sea_mask.astype(BF16)[None]).transpose(1, 2, 0)
    grad_f = grad_out.astype(F32)
    scaled_grad = (
        (ocean_f * layer_scale[:, None, None] * grad_f)
        .astype(BF16)
        .transpose(1, 2, 0)
        .reshape(cells, chans)
    )
    sg_all = lax.all_gather(scaled_grad, "ch", axis=0, tiled=False)
    taps = jnp.pad(kernel.reshape(chans, 49).T, ((0, 7), (0, 0)))

    west, east, tops = edges(masked, None, 0)
    mix, ext = pl.pallas_call(
        functools.partial(conv_kernel, tiles),
        out_shape=[
            jax.ShapeDtypeStruct((cols, rows, chans), F32),
            jax.ShapeDtypeStruct((cols + 6, rows + 16, chans), F32),
        ],
        in_specs=[SMEM_SPEC, SMEM_SPEC] + [VMEM_SPEC] * 5,
        out_specs=[VMEM_SPEC] * 2,
        scratch_shapes=[pltpu.VMEM((7, cols + 6, rows, chans), F32)],
        compiler_params=plain,
    )(mine, fold_partner, masked, west, east, tops, taps)

    branch, mg, gw_in, gw_out = middle(
        mix.reshape(cells, chans),
        sg_all,
        w_in.reshape(n, chans, hid),
        w_out.reshape(hid, n, chans).transpose(1, 0, 2),
        ln_gain.reshape(n, 1, chans),
        ln_shift.reshape(n, 1, chans),
        factor,
    )
    mg = mg.reshape(cols, rows, chans)
    tap_sums, half = pl.pallas_call(
        tap_grad_kernel,
        out_shape=[
            jax.ShapeDtypeStruct((56, chans), F32),
            jax.ShapeDtypeStruct((cols, rows, chans), BF16),
        ],
        in_specs=[VMEM_SPEC] * 2,
        out_specs=[VMEM_SPEC] * 2,
        scratch_shapes=[
            pltpu.VMEM((7, cols + 6, rows, chans), F32),
            pltpu.VMEM((49, 8, chans), F32),
        ],
        compiler_params=plain,
    )(ext, mg)
    west, east, tops, extras = edges(half, tap_sums, 2)
    field_grad, kernel_total = pl.pallas_call(
        functools.partial(spread_kernel, tiles),
        out_shape=[
            jax.ShapeDtypeStruct((cols, rows, chans), F32),
            jax.ShapeDtypeStruct((56, chans), F32),
        ],
        in_specs=[SMEM_SPEC, SMEM_SPEC] + [VMEM_SPEC] * 6,
        out_specs=[VMEM_SPEC] * 2,
        scratch_shapes=[
            pltpu.VMEM((cols + 6, rows + 16, chans), F32),
            pltpu.VMEM((7, cols + 6, rows, chans), F32),
            pltpu.VMEM((3, cols + 6, 8, chans), F32),
        ],
        compiler_params=plain,
    )(mine, fold_partner, mg, west, east, tops, taps, extras)

    block_out = (
        ocean_f
        * (
            field_in.astype(F32)
            + layer_scale[:, None, None] * branch.T.reshape(chans, cols, rows)
        )
    ).astype(BF16)
    grad_x = (ocean_f * (grad_f + field_grad.transpose(2, 0, 1))).astype(BF16)
    kernel_grad = kernel_total[:49].T.reshape(chans, 7, 7) * factor
    return (block_out, grad_x, kernel_grad, gw_in, gw_out)


def solution(mesh):
    placed = (
        P("ch", ("grp", "lon"), None),
        P("lon", None),
        P(),
        P("ch", None, None),
        P(),
        P(),
        P(None, "ch"),
        P("ch", None),
        P("ch"),
        P("ch", ("grp", "lon"), None),
    )
    return jax.shard_map(
        body,
        mesh=mesh,
        in_specs=placed,
        out_specs=(
            P("ch", ("grp", "lon"), None),
            P("ch", ("grp", "lon"), None),
            P(("grp", "ch"), None, None),
            P("grp", "ch"),
            P(("grp", "ch"), None),
        ),
        check_vma=False,
    )
```

```python
import functools
import math

import jax
import jax.numpy as jnp
from jax import lax
from jax.experimental import pallas as pl
from jax.experimental.pallas import tpu as pltpu
from jax.sharding import PartitionSpec as P

EPSILON = 1e-06
F32 = jnp.float32
BF16 = jnp.bfloat16
MESH = pl.DeviceIdType.MESH
VMEM_SPEC = pl.BlockSpec(memory_space=pltpu.VMEM)
SMEM_SPEC = pl.BlockSpec(memory_space=pltpu.SMEM)
LIMIT = 48 * 1024 * 1024


def greet(axes):
    barrier = pltpu.get_barrier_semaphore()
    total = 0
    for axis in axes:
        count = lax.axis_size(axis)
        me = lax.axis_index(axis)
        for d in range(1, count):
            pl.semaphore_signal(
                barrier, inc=1, device_id={axis: lax.rem(me + d, count)}, device_id_type=MESH
            )
        total += count - 1
    pl.semaphore_wait(barrier, total)


def push(src, dst, sems, slot, axis, target):
    copy = pltpu.make_async_remote_copy(
        src_ref=src,
        dst_ref=dst,
        send_sem=sems[0].at[slot],
        recv_sem=sems[1].at[slot],
        device_id={axis: target},
        device_id_type=MESH,
    )
    copy.start()
    return copy


def gelu_parts(hidden):
    normal_cdf = 0.5 * (1.0 + lax.erf(hidden * (1.0 / math.sqrt(2.0))))
    density = jnp.exp(-0.5 * hidden * hidden) * (1.0 / math.sqrt(2.0 * math.pi))
    return (hidden * normal_cdf, normal_cdf + hidden * density)


def dot(a, b, dims):
    return lax.dot_general(a, b, (dims, ((), ())), preferred_element_type=F32)


def fill_shifts(ext_ref, shifts_ref, rows):
    def one(q, _):
        for b in range(7):
            shifts_ref[b, q] = ext_ref[q, pl.ds(5 + b, rows)]
        return 0

    lax.fori_loop(0, ext_ref.shape[0], one, 0)


def send_edges(x_ref, pack, west, east, tops, sems, me, tiles):
    cols, rows, chans = x_ref.shape
    right, left = lax.rem(me + 1, tiles), lax.rem(me + tiles - 1, tiles)
    copies = [
        push(x_ref.at[pl.ds(cols - 3, 3)], west, sems, 0, "lon", right),
        push(x_ref.at[pl.ds(0, 3)], east, sems, tiles, "lon", left),
    ]
    for col in range(cols):
        top = x_ref[col, pl.ds(rows - 16, 16)].astype(F32)
        for k in range(3):
            pack[pl.ds(col * 3 + k, 1)] = top[15 - k : 16 - k]
    tops[me] = pack[...].astype(BF16)
    for d in range(1, tiles):
        t = lax.rem(me + d, tiles)
        copies.append(push(tops.at[me], tops.at[me], sems, d, "lon", t))
    return copies


def mega_kernel(n, tiles, factor, block,
                partner_ref, x_ref, sg_ref, tap_ref, win_ref, wout_all, gain_ref, shift_ref,
                branch_ref, fg_ref, kernel_ref, agi, ago,
                ext_ref, shifts_ref, fold_ref, pack, west, east, tops, west2, east2, tops2,
                half_ref, sums_ref, extras_ref, extra_ref, wout_ref, mix_ref, sgg,
                mixg, normed, act, agrad, hg, mean, inv, own_ng, one_acc, two_acc,
                nsend, nrecv, bsend, brecv, psend, precv,
                gof, gif, gsi, gri, gso, gro,
                *sem_refs):
    cols, rows, chans = x_ref.shape
    cells = cols * rows
    hid = win_ref.shape[2]
    width = n * chans
    blocks = cells // block
    (m_sems, n_sems, p_sems, b_sems, s_sems, i_sems, o_sems, ai_sems, ao_sems, k_sems,
     e_sems, f_sems) = [(sem_refs[2 * k], sem_refs[2 * k + 1]) for k in range(12)]
    me = lax.axis_index("ch")
    lon = lax.axis_index("lon")
    greet(("ch", "lon"))
    peers = [lax.rem(me + d, n) for d in range(n)]
    spans = [lax.rem(lon + d, tiles) for d in range(tiles)]

    def loop(step):
        def one(i, _):
            step(pl.ds(pl.multiple_of(i * block, block), block))
            return 0

        lax.fori_loop(0, blocks, one, 0)

    pack[...] = jnp.zeros_like(pack)
    ecopies = send_edges(x_ref, pack, west, east, tops, e_sems, lon, tiles)
    scopies = [push(sg_ref, sgg.at[me], s_sems, d, "ch", peers[d]) for d in range(1, n)]
    sgg[me] = sg_ref[...]
    for j in range(n):
        wout_ref[j] = wout_all[:, j * chans : (j + 1) * chans]
    ext_ref[...] = jnp.zeros_like(ext_ref)
    fold_ref[...] = jnp.zeros_like(fold_ref)
    for q in range(cols):
        ext_ref[q + 3, pl.ds(8, rows)] = x_ref[q].astype(F32)
    for copy in ecopies:
        copy.wait()

    for q in range(3):
        ext_ref[q, pl.ds(8, rows)] = west[q].astype(F32)
        ext_ref[cols + 3 + q, pl.ds(8, rows)] = east[q].astype(F32)
    for step in (-1, 0, 1):
        tile = lax.rem(lon + step + tiles, tiles)
        top = tops[partner_ref[tile]].astype(F32)
        for q in range(cols + 6):
            if (q - 3) // cols == step:
                base = (cols - 1 - (q - 3) % cols) * 3
                ext_ref[q, pl.ds(8 + rows, 3)] = top[base : base + 3]
    fill_shifts(ext_ref, shifts_ref, rows)

    def conv(i, _):
        acc = jnp.zeros((rows, chans), F32)
        for a in range(7):
            for b in range(7):
                acc = acc + tap_ref[pl.ds(a * 7 + b, 1)] * shifts_ref[b, i + a]
        cut = pl.ds(pl.multiple_of(i * rows, rows), rows)
        mix_ref[cut] = acc
        mixg[me, cut] = acc.astype(BF16)
        return 0

    lax.fori_loop(0, cols, conv, 0)
    mcopies = [
        push(mixg.at[me], mixg.at[me], m_sems, d, "ch", peers[d]) for d in range(1, n)
    ]
    for copy in scopies:
        copy.wait()

    def grads(cut):
        total = dot(sgg[0, cut], wout_ref[0], ((1,), (1,)))
        for j in range(1, n):
            total = total + dot(sgg[j, cut], wout_ref[j], ((1,), (1,)))
        agrad[cut] = total

    loop(grads)
    for copy in mcopies:
        copy.wait()

    def forward(cut):
        parts = [mixg[j, cut].astype(F32) for j in range(n)]
        one = functools.reduce(jnp.add, parts)
        two = functools.reduce(jnp.add, [v * v for v in parts])
        mean_cell = jnp.sum(one, axis=1, keepdims=True) / width
        sigma = lax.rsqrt(
            jnp.sum(two, axis=1, keepdims=True) / width - mean_cell * mean_cell + EPSILON
        )
        mean[cut] = mean_cell
        inv[cut] = sigma
        hidden = jnp.zeros((block, hid), F32)
        for j in range(n):
            value = ((parts[j] - mean_cell) * sigma * gain_ref[j] + shift_ref[j]).astype(BF16)
            normed[j, cut] = value
            hidden = hidden + dot(value, win_ref[j], ((1,), (0,)))
        activation, slope = gelu_parts(hidden)
        act[cut] = activation.astype(BF16)
        hg[cut] = (agrad[cut] * slope).astype(BF16)
        one_acc[cut] = jnp.zeros((block, chans), F32)
        two_acc[cut] = jnp.zeros((block, chans), F32)

    loop(forward)

    ro, ri = n * hid // tiles, width // tiles
    for j in range(n):
        part = dot(act[...], sgg[j], ((0,), (0,)))
        gof[pl.ds(j * hid, hid)] = part
        gso[pl.ds(j * hid, hid)] = part.astype(BF16)
    ocopies, icopies = [], []
    for d in range(1, tiles):
        src = gso.at[pl.ds(pl.multiple_of(spans[d] * ro, ro), ro)]
        ocopies.append(push(src, gro.at[d], o_sems, d, "lon", spans[d]))

    ncopies = []
    for d in list(range(1, n)) + [0]:
        t = peers[d]

        def back(cut, d=d, t=t):
            part = dot(hg[cut], win_ref[t], ((1,), (1,)))
            if d:
                nsend[d, cut] = part.astype(BF16)
            else:
                own_ng[cut] = part
            scaled = part * gain_ref[t]
            centred = (mixg[t, cut].astype(F32) - mean[cut]) * inv[cut]
            one_acc[cut] += scaled
            two_acc[cut] += scaled * centred

        loop(back)
        if d:
            ncopies.append(push(nsend.at[d], nrecv.at[d], n_sems, d, "ch", t))
    lane = lax.broadcasted_iota(jnp.int32, (cells, 128), 1)
    pair = jnp.where(
        lane == 0,
        jnp.sum(one_acc[...], axis=1, keepdims=True),
        jnp.sum(two_acc[...], axis=1, keepdims=True),
    )
    psend[...] = pair.T[:8]
    pcopies = [push(psend, precv.at[d], p_sems, d, "ch", peers[d]) for d in range(1, n)]

    for j in range(n):
        part = dot(normed[j], hg[...], ((0,), (0,)))
        gif[pl.ds(j * chans, chans)] = part
        gsi[pl.ds(j * chans, chans)] = part.astype(BF16)
    for d in range(1, tiles):
        src = gsi.at[pl.ds(pl.multiple_of(spans[d] * ri, ri), ri)]
        icopies.append(push(src, gri.at[d], i_sems, d, "lon", spans[d]))

    bcopies = []
    for d in range(1, n):
        t = peers[d]

        def out(cut, d=d, t=t):
            bsend[d, cut] = dot(act[cut], wout_ref[t], ((1,), (0,))).astype(BF16)

        loop(out)
        bcopies.append(push(bsend.at[d], brecv.at[d], b_sems, d, "ch", t))

    def out_own(cut):
        branch_ref[cut] = dot(act[cut], wout_ref[me], ((1,), (0,)))

    loop(out_own)

    for copy in pcopies + ncopies:
        copy.wait()
    sums = psend[...]
    for d in range(1, n):
        sums = sums + precv[d]
    both = jnp.concatenate([sums, jnp.zeros((120, cells), F32)], axis=0).T
    one_mean = both[:, 0:1] / width
    two_mean = both[:, 1:2] / width
    total = own_ng[...]
    for d in range(1, n):
        total = total + nrecv[d].astype(F32)
    centred = (mix_ref[...] - mean[...]) * inv[...]
    own_ng[...] = inv[...] * (total * gain_ref[me] - one_mean - centred * two_mean)
    half_ref[...] = own_ng[...].astype(BF16).reshape(cols, rows, chans)
    fcopies = send_edges(half_ref, pack, west2, east2, tops2, f_sems, lon, tiles)

    acopies = []
    for copies, own, recv, held, size, sems in (
        (ocopies, gof, gro, ago, ro, ao_sems),
        (icopies, gif, gri, agi, ri, ai_sems),
    ):
        for copy in copies:
            copy.wait()
        total = own[pl.ds(pl.multiple_of(lon * size, size), size)]
        for d in range(1, tiles):
            total = total + recv[d].astype(F32)
        held[lon] = (total * factor).astype(BF16)
        for d in range(1, tiles):
            acopies.append(push(held.at[lon], held.at[lon], sems, d, "lon", spans[d]))

    sums_ref[...] = jnp.zeros_like(sums_ref)
    extra_ref[...] = jnp.zeros_like(extra_ref)

    def tap_grad(i, _):
        mg = own_ng[pl.ds(pl.multiple_of(i * rows, rows), rows)]
        for a in range(7):
            for b in range(7):
                prod = shifts_ref[b, i + a] * mg
                sums_ref[a * 7 + b] += jnp.sum(prod.reshape(rows // 8, 8, chans), axis=0)
        return 0

    lax.fori_loop(0, cols, tap_grad, 0)
    for t in range(49):
        extra_ref[pl.ds(t, 1)] = jnp.sum(sums_ref[t], axis=0, keepdims=True)
    kcopies = [
        push(extra_ref, extras_ref.at[lon], k_sems, d, "lon", spans[d])
        for d in range(1, tiles)
    ]
    extras_ref[lon] = extra_ref[...]

    for q in range(cols):
        ext_ref[q + 3, pl.ds(8, rows)] = own_ng[pl.ds(q * rows, rows)]
    for q in range(cols + 6):
        ext_ref[q, pl.ds(8 + rows, 8)] = jnp.zeros((8, chans), F32)
    for copy in fcopies:
        copy.wait()
    for q in range(3):
        ext_ref[q, pl.ds(8, rows)] = west2[q].astype(F32)
        ext_ref[cols + 3 + q, pl.ds(8, rows)] = east2[q].astype(F32)
    for step in (-1, 0, 1):
        tile = lax.rem(partner_ref[lon] + step + tiles, tiles)
        top = tops2[tile].astype(F32)
        for q in range(cols + 6):
            if (q - 3) // cols == step:
                base = (q - 3) % cols * 3
                for s in range(3):
                    fold_ref[s, q, pl.ds(5 + s, 3 - s)] = top[base : base + 3 - s]
    fill_shifts(ext_ref, shifts_ref, rows)

    def spread(i, _):
        acc = jnp.zeros((rows, chans), F32)
        for a in range(7):
            for b in range(7):
                acc = acc + tap_ref[pl.ds(a * 7 + b, 1)] * shifts_ref[6 - b, i + 6 - a]
        fg_ref[i] = acc
        north = jnp.zeros((8, chans), F32)
        for a in range(7):
            for s in range(3):
                north = north + tap_ref[pl.ds(a * 7 + 6 - s, 1)] * fold_ref[
                    s, cols - 1 - i + 6 - a
                ]
        fg_ref[i, pl.ds(rows - 8, 8)] += north
        return 0

    lax.fori_loop(0, cols, spread, 0)

    for copy in bcopies:
        copy.wait()
    total = branch_ref[...]
    for d in range(1, n):
        total = total + brecv[d].astype(F32)
    branch_ref[...] = total
    for copy in kcopies:
        copy.wait()
    kernel_ref[...] = jnp.sum(extras_ref[...], axis=0)
    for copy in acopies:
        copy.wait()


def mega(partner, x, sg, taps, win, wout, gain, shift, factor):
    cols, rows, chans = x.shape
    cells = cols * rows
    n, _, hid = win.shape
    tiles = lax.axis_size("lon")
    width = n * chans
    ro, ri = n * hid // tiles, width // tiles
    top_rows = -(-cols * 3 // 16) * 16
    S = pltpu.VMEM
    scratch = [
        S((cols + 6, rows + 16, chans), F32), S((7, cols + 6, rows, chans), F32),
        S((3, cols + 6, 8, chans), F32), S((top_rows, chans), F32),
        S((3, rows, chans), BF16), S((3, rows, chans), BF16), S((tiles, top_rows, chans), BF16),
        S((3, rows, chans), BF16), S((3, rows, chans), BF16), S((tiles, top_rows, chans), BF16),
        S((cols, rows, chans), BF16), S((49, 8, chans), F32),
        S((tiles, 56, chans), F32), S((56, chans), F32),
        S((n, hid, chans), BF16), S((cells, chans), F32), S((n, cells, chans), BF16),
        S((n, cells, chans), BF16), S((n, cells, chans), BF16),
        S((cells, hid), BF16), S((cells, hid), F32), S((cells, hid), BF16),
        S((cells, 1), F32), S((cells, 1), F32), S((cells, chans), F32),
        S((cells, chans), F32), S((cells, chans), F32),
        S((n, cells, chans), BF16), S((n, cells, chans), BF16),
        S((n, cells, chans), BF16), S((n, cells, chans), BF16),
        S((8, cells), F32), S((n, 8, cells), F32),
        S((n * hid, chans), F32), S((width, hid), F32),
        S((width, hid), BF16), S((tiles, ri, hid), BF16),
        S((n * hid, chans), BF16), S((tiles, ro, chans), BF16),
    ]
    for count in (n,) * 5 + (tiles,) * 5 + (tiles + 1,) * 2:
        scratch += [pltpu.SemaphoreType.DMA((count,)), pltpu.SemaphoreType.DMA((count,))]
    return pl.pallas_call(
        functools.partial(mega_kernel, n, tiles, factor, 256),
        out_shape=[
            jax.ShapeDtypeStruct((cells, chans), F32),
            jax.ShapeDtypeStruct((cols, rows, chans), F32),
            jax.ShapeDtypeStruct((56, chans), F32),
            jax.ShapeDtypeStruct((tiles, ri, hid), BF16),
            jax.ShapeDtypeStruct((tiles, ro, chans), BF16),
        ],
        in_specs=[SMEM_SPEC] + [VMEM_SPEC] * 7,
        out_specs=[VMEM_SPEC] * 5,
        scratch_shapes=scratch,
        compiler_params=pltpu.CompilerParams(
            collective_id=1, has_side_effects=True, vmem_limit_bytes=LIMIT
        ),
    )(partner, x, sg, taps, win, wout, gain, shift)


def body(
    field_in, sea_mask, fold_partner, kernel, ln_gain, ln_shift, w_in, w_out, layer_scale, grad_out
):
    chans, cols, rows = field_in.shape
    tiles = lax.axis_size("lon")
    n = lax.axis_size("ch")
    cells = cols * rows
    hid = w_in.shape[1]
    factor = 1.0 / math.sqrt(tiles * cells)

    ocean_f = sea_mask.astype(F32)[None]
    masked = (field_in * sea_mask.astype(BF16)[None]).transpose(1, 2, 0)
    grad_f = grad_out.astype(F32)
    scaled_grad = (
        (ocean_f * layer_scale[:, None, None] * grad_f)
        .astype(BF16)
        .transpose(1, 2, 0)
        .reshape(cells, chans)
    )
    taps = jnp.pad(kernel.reshape(chans, 49).T, ((0, 7), (0, 0)))
    branch, field_grad, kernel_total, gw_in, gw_out = mega(
        fold_partner,
        masked,
        scaled_grad,
        taps,
        w_in.reshape(n, chans, hid),
        w_out,
        ln_gain.reshape(n, 1, chans),
        ln_shift.reshape(n, 1, chans),
        factor,
    )
    block_out = (
        ocean_f
        * (
            field_in.astype(F32)
            + layer_scale[:, None, None] * branch.T.reshape(chans, cols, rows)
        )
    ).astype(BF16)
    grad_x = (ocean_f * (grad_f + field_grad.transpose(2, 0, 1))).astype(BF16)
    kernel_grad = kernel_total[:49].T.reshape(chans, 7, 7) * factor
    gw_in = gw_in.reshape(n * chans, hid).astype(F32)
    gw_out = gw_out.reshape(n, hid, chans).transpose(1, 0, 2).reshape(hid, n * chans).astype(F32)
    return (block_out, grad_x, kernel_grad, gw_in, gw_out)


def solution(mesh):
    placed = (
        P("ch", ("grp", "lon"), None),
        P("lon", None),
        P(),
        P("ch", None, None),
        P(),
        P(),
        P(None, "ch"),
        P("ch", None),
        P("ch"),
        P("ch", ("grp", "lon"), None),
    )
    return jax.shard_map(
        body,
        mesh=mesh,
        in_specs=placed,
        out_specs=(
            P("ch", ("grp", "lon"), None),
            P("ch", ("grp", "lon"), None),
            P(("grp", "ch"), None, None),
            P("grp", "ch"),
            P(("grp", "ch"), None),
        ),
        check_vma=False,
    )
```

```python
import functools
import math

import jax
import jax.numpy as jnp
from jax import lax
from jax.experimental import pallas as pl
from jax.experimental.pallas import tpu as pltpu
from jax.sharding import PartitionSpec as P

EPSILON = 1e-06
F32 = jnp.float32
BF16 = jnp.bfloat16
MESH = pl.DeviceIdType.MESH
VMEM_SPEC = pl.BlockSpec(memory_space=pltpu.VMEM)
SMEM_SPEC = pl.BlockSpec(memory_space=pltpu.SMEM)
LIMIT = 48 * 1024 * 1024


def greet(axes):
    barrier = pltpu.get_barrier_semaphore()
    total = 0
    for axis in axes:
        count = lax.axis_size(axis)
        me = lax.axis_index(axis)
        for d in range(1, count):
            pl.semaphore_signal(
                barrier, inc=1, device_id={axis: lax.rem(me + d, count)}, device_id_type=MESH
            )
        total += count - 1
    pl.semaphore_wait(barrier, total)


def push(src, dst, sems, slot, axis, target):
    copy = pltpu.make_async_remote_copy(
        src_ref=src,
        dst_ref=dst,
        send_sem=sems[0].at[slot],
        recv_sem=sems[1].at[slot],
        device_id={axis: target},
        device_id_type=MESH,
    )
    copy.start()
    return copy


def gelu_parts(hidden):
    normal_cdf = 0.5 * (1.0 + lax.erf(hidden * (1.0 / math.sqrt(2.0))))
    density = jnp.exp(-0.5 * hidden * hidden) * (1.0 / math.sqrt(2.0 * math.pi))
    return (hidden * normal_cdf, normal_cdf + hidden * density)


def dot(a, b, dims):
    return lax.dot_general(a, b, (dims, ((), ())), preferred_element_type=F32)


def fill_shifts(ext_ref, shifts_ref, rows):
    def one(q, _):
        for b in range(7):
            shifts_ref[b, q] = ext_ref[q, pl.ds(5 + b, rows)]
        return 0

    lax.fori_loop(0, ext_ref.shape[0], one, 0)


def send_edges(x_ref, pack, west, east, tops, sems, me, tiles):
    cols, rows, chans = x_ref.shape
    right, left = lax.rem(me + 1, tiles), lax.rem(me + tiles - 1, tiles)
    copies = [
        push(x_ref.at[pl.ds(cols - 3, 3)], west, sems, 0, "lon", right),
        push(x_ref.at[pl.ds(0, 3)], east, sems, tiles, "lon", left),
    ]
    for col in range(cols):
        top = x_ref[col, pl.ds(rows - 16, 16)].astype(F32)
        for k in range(3):
            pack[pl.ds(col * 3 + k, 1)] = top[15 - k : 16 - k]
    tops[me] = pack[...].astype(BF16)
    for d in range(1, tiles):
        t = lax.rem(me + d, tiles)
        copies.append(push(tops.at[me], tops.at[me], sems, d, "lon", t))
    return copies


def mega_kernel(n, tiles, factor, block,
                partner_ref, x_ref, sg_ref, tap_ref, win_ref, wout_all, gain_ref, shift_ref,
                branch_ref, fg_ref, kernel_ref, agi, ago,
                ext_ref, shifts_ref, fold_ref, pack, west, east, tops, west2, east2, tops2,
                half_ref, sums_ref, extras_ref, extra_ref, wout_ref, mix_ref, sgg,
                mixg, normed, act, agrad, hg, mean, inv, own_ng, one_acc, two_acc,
                nsend, nrecv, bsend, brecv, psend, precv,
                gof, gif, gsi, gri, gso, gro,
                *sem_refs):
    cols, rows, chans = x_ref.shape
    cells = cols * rows
    hid = win_ref.shape[2]
    width = n * chans
    blocks = cells // block
    (m_sems, n_sems, p_sems, b_sems, s_sems, i_sems, o_sems, ai_sems, ao_sems, k_sems,
     e_sems, f_sems) = [(sem_refs[2 * k], sem_refs[2 * k + 1]) for k in range(12)]
    me = lax.axis_index("ch")
    lon = lax.axis_index("lon")
    greet(("ch", "lon"))
    chips = n // 2
    chip, core = me // 2, lax.rem(me, 2)
    peers = [
        lax.rem(chip + d // 2, chips) * 2 + lax.rem(core + d % 2, 2) for d in range(n)
    ]
    far_first = list(range(2, n)) + [1]
    spans = [lax.rem(lon + d, tiles) for d in range(tiles)]

    def loop(step):
        def one(i, _):
            step(pl.ds(pl.multiple_of(i * block, block), block))
            return 0

        lax.fori_loop(0, blocks, one, 0)

    pack[...] = jnp.zeros_like(pack)
    ecopies = send_edges(x_ref, pack, west, east, tops, e_sems, lon, tiles)
    scopies = [push(sg_ref, sgg.at[me], s_sems, d, "ch", peers[d]) for d in range(1, n)]
    sgg[me] = sg_ref[...]
    for j in range(n):
        wout_ref[j] = wout_all[:, j * chans : (j + 1) * chans]
    ext_ref[...] = jnp.zeros_like(ext_ref)
    fold_ref[...] = jnp.zeros_like(fold_ref)
    for q in range(cols):
        ext_ref[q + 3, pl.ds(8, rows)] = x_ref[q].astype(F32)
    for copy in ecopies:
        copy.wait()

    for q in range(3):
        ext_ref[q, pl.ds(8, rows)] = west[q].astype(F32)
        ext_ref[cols + 3 + q, pl.ds(8, rows)] = east[q].astype(F32)
    for step in (-1, 0, 1):
        tile = lax.rem(lon + step + tiles, tiles)
        top = tops[partner_ref[tile]].astype(F32)
        for q in range(cols + 6):
            if (q - 3) // cols == step:
                base = (cols - 1 - (q - 3) % cols) * 3
                ext_ref[q, pl.ds(8 + rows, 3)] = top[base : base + 3]
    fill_shifts(ext_ref, shifts_ref, rows)

    def conv(i, _):
        acc = jnp.zeros((rows, chans), F32)
        for a in range(7):
            for b in range(7):
                acc = acc + tap_ref[pl.ds(a * 7 + b, 1)] * shifts_ref[b, i + a]
        cut = pl.ds(pl.multiple_of(i * rows, rows), rows)
        mix_ref[cut] = acc
        mixg[me, cut] = acc.astype(BF16)
        return 0

    def push_block(owner, k, slot, target):
        view = mixg.at[owner, pl.ds(k * block, block)]
        return push(view, view, m_sems, slot * blocks + k, "ch", target)

    near, far = [], []
    per = cols // blocks
    for k in range(blocks):
        lax.fori_loop(k * per, (k + 1) * per, conv, 0)
        far.append([push_block(me, k, c, peers[2 * c]) for c in range(1, chips)])
        near.append([push_block(me, k, 0, peers[1])])
    for copy in scopies:
        copy.wait()

    def grads(cut):
        total = dot(sgg[0, cut], wout_ref[0], ((1,), (1,)))
        for j in range(1, n):
            total = total + dot(sgg[j, cut], wout_ref[j], ((1,), (1,)))
        agrad[cut] = total

    loop(grads)

    def forward(cut):
        parts = [mixg[j, cut].astype(F32) for j in range(n)]
        one = functools.reduce(jnp.add, parts)
        two = functools.reduce(jnp.add, [v * v for v in parts])
        mean_cell = jnp.sum(one, axis=1, keepdims=True) / width
        sigma = lax.rsqrt(
            jnp.sum(two, axis=1, keepdims=True) / width - mean_cell * mean_cell + EPSILON
        )
        mean[cut] = mean_cell
        inv[cut] = sigma
        hidden = jnp.zeros((block, hid), F32)
        for j in range(n):
            value = ((parts[j] - mean_cell) * sigma * gain_ref[j] + shift_ref[j]).astype(BF16)
            normed[j, cut] = value
            hidden = hidden + dot(value, win_ref[j], ((1,), (0,)))
        activation, slope = gelu_parts(hidden)
        act[cut] = activation.astype(BF16)
        hg[cut] = (agrad[cut] * slope).astype(BF16)
        one_acc[cut] = jnp.zeros((block, chans), F32)
        two_acc[cut] = jnp.zeros((block, chans), F32)

    for k in range(blocks):
        for c in range(1, chips):
            far[k][c - 1].wait()
            owner = lax.rem(chip - c + chips, chips) * 2 + core
            near[k].append(push_block(owner, k, chips - 1 + c, peers[1]))
        for copy in near[k]:
            copy.wait()
        forward(pl.ds(k * block, block))

    ro, ri = n * hid // tiles, width // tiles
    for j in range(n):
        part = dot(act[...], sgg[j], ((0,), (0,)))
        gof[pl.ds(j * hid, hid)] = part
        gso[pl.ds(j * hid, hid)] = part.astype(BF16)
    ocopies, icopies = [], []
    for d in range(1, tiles):
        src = gso.at[pl.ds(pl.multiple_of(spans[d] * ro, ro), ro)]
        ocopies.append(push(src, gro.at[d], o_sems, d, "lon", spans[d]))

    ncopies = []
    for d in far_first + [0]:
        t = peers[d]

        def back(cut, d=d, t=t):
            part = dot(hg[cut], win_ref[t], ((1,), (1,)))
            if d:
                nsend[d, cut] = part.astype(BF16)
            else:
                own_ng[cut] = part
            scaled = part * gain_ref[t]
            centred = (mixg[t, cut].astype(F32) - mean[cut]) * inv[cut]
            one_acc[cut] += scaled
            two_acc[cut] += scaled * centred

        loop(back)
        if d:
            ncopies.append(push(nsend.at[d], nrecv.at[d], n_sems, d, "ch", t))
    lane = lax.broadcasted_iota(jnp.int32, (cells, 128), 1)
    pair = jnp.where(
        lane == 0,
        jnp.sum(one_acc[...], axis=1, keepdims=True),
        jnp.sum(two_acc[...], axis=1, keepdims=True),
    )
    psend[...] = pair.T[:8]
    pcopies = [push(psend, precv.at[d], p_sems, d, "ch", peers[d]) for d in range(1, n)]

    for j in range(n):
        part = dot(normed[j], hg[...], ((0,), (0,)))
        gif[pl.ds(j * chans, chans)] = part
        gsi[pl.ds(j * chans, chans)] = part.astype(BF16)
    for d in range(1, tiles):
        src = gsi.at[pl.ds(pl.multiple_of(spans[d] * ri, ri), ri)]
        icopies.append(push(src, gri.at[d], i_sems, d, "lon", spans[d]))

    bcopies = []
    for d in far_first:
        t = peers[d]

        def out(cut, d=d, t=t):
            bsend[d, cut] = dot(act[cut], wout_ref[t], ((1,), (0,))).astype(BF16)

        loop(out)
        bcopies.append(push(bsend.at[d], brecv.at[d], b_sems, d, "ch", t))

    def out_own(cut):
        branch_ref[cut] = dot(act[cut], wout_ref[me], ((1,), (0,)))

    loop(out_own)

    for copy in pcopies + ncopies:
        copy.wait()
    sums = psend[...]
    for d in range(1, n):
        sums = sums + precv[d]
    both = jnp.concatenate([sums, jnp.zeros((120, cells), F32)], axis=0).T
    one_mean = both[:, 0:1] / width
    two_mean = both[:, 1:2] / width
    total = own_ng[...]
    for d in range(1, n):
        total = total + nrecv[d].astype(F32)
    centred = (mix_ref[...] - mean[...]) * inv[...]
    own_ng[...] = inv[...] * (total * gain_ref[me] - one_mean - centred * two_mean)
    half_ref[...] = own_ng[...].astype(BF16).reshape(cols, rows, chans)
    fcopies = send_edges(half_ref, pack, west2, east2, tops2, f_sems, lon, tiles)

    acopies = []
    for copies, own, recv, held, size, sems in (
        (ocopies, gof, gro, ago, ro, ao_sems),
        (icopies, gif, gri, agi, ri, ai_sems),
    ):
        for copy in copies:
            copy.wait()
        total = own[pl.ds(pl.multiple_of(lon * size, size), size)]
        for d in range(1, tiles):
            total = total + recv[d].astype(F32)
        held[lon] = (total * factor).astype(BF16)
        for d in range(1, tiles):
            acopies.append(push(held.at[lon], held.at[lon], sems, d, "lon", spans[d]))

    sums_ref[...] = jnp.zeros_like(sums_ref)
    extra_ref[...] = jnp.zeros_like(extra_ref)

    def tap_grad(i, _):
        mg = own_ng[pl.ds(pl.multiple_of(i * rows, rows), rows)]
        for a in range(7):
            for b in range(7):
                prod = shifts_ref[b, i + a] * mg
                sums_ref[a * 7 + b] += jnp.sum(prod.reshape(rows // 8, 8, chans), axis=0)
        return 0

    lax.fori_loop(0, cols, tap_grad, 0)
    for t in range(49):
        extra_ref[pl.ds(t, 1)] = jnp.sum(sums_ref[t], axis=0, keepdims=True)
    kcopies = [
        push(extra_ref, extras_ref.at[lon], k_sems, d, "lon", spans[d])
        for d in range(1, tiles)
    ]
    extras_ref[lon] = extra_ref[...]

    for q in range(cols):
        ext_ref[q + 3, pl.ds(8, rows)] = own_ng[pl.ds(q * rows, rows)]
    for q in range(cols + 6):
        ext_ref[q, pl.ds(8 + rows, 8)] = jnp.zeros((8, chans), F32)
    for copy in fcopies:
        copy.wait()
    for q in range(3):
        ext_ref[q, pl.ds(8, rows)] = west2[q].astype(F32)
        ext_ref[cols + 3 + q, pl.ds(8, rows)] = east2[q].astype(F32)
    for step in (-1, 0, 1):
        tile = lax.rem(partner_ref[lon] + step + tiles, tiles)
        top = tops2[tile].astype(F32)
        for q in range(cols + 6):
            if (q - 3) // cols == step:
                base = (q - 3) % cols * 3
                for s in range(3):
                    fold_ref[s, q, pl.ds(5 + s, 3 - s)] = top[base : base + 3 - s]
    fill_shifts(ext_ref, shifts_ref, rows)

    def spread(i, _):
        acc = jnp.zeros((rows, chans), F32)
        for a in range(7):
            for b in range(7):
                acc = acc + tap_ref[pl.ds(a * 7 + b, 1)] * shifts_ref[6 - b, i + 6 - a]
        fg_ref[i] = acc
        north = jnp.zeros((8, chans), F32)
        for a in range(7):
            for s in range(3):
                north = north + tap_ref[pl.ds(a * 7 + 6 - s, 1)] * fold_ref[
                    s, cols - 1 - i + 6 - a
                ]
        fg_ref[i, pl.ds(rows - 8, 8)] += north
        return 0

    lax.fori_loop(0, cols, spread, 0)

    for copy in bcopies:
        copy.wait()
    total = branch_ref[...]
    for d in range(1, n):
        total = total + brecv[d].astype(F32)
    branch_ref[...] = total
    for copy in kcopies:
        copy.wait()
    kernel_ref[...] = jnp.sum(extras_ref[...], axis=0)
    for copy in acopies:
        copy.wait()


def mega(partner, x, sg, taps, win, wout, gain, shift, factor):
    cols, rows, chans = x.shape
    cells = cols * rows
    n, _, hid = win.shape
    tiles = lax.axis_size("lon")
    width = n * chans
    ro, ri = n * hid // tiles, width // tiles
    top_rows = -(-cols * 3 // 16) * 16
    S = pltpu.VMEM
    scratch = [
        S((cols + 6, rows + 16, chans), F32), S((7, cols + 6, rows, chans), F32),
        S((3, cols + 6, 8, chans), F32), S((top_rows, chans), F32),
        S((3, rows, chans), BF16), S((3, rows, chans), BF16), S((tiles, top_rows, chans), BF16),
        S((3, rows, chans), BF16), S((3, rows, chans), BF16), S((tiles, top_rows, chans), BF16),
        S((cols, rows, chans), BF16), S((49, 8, chans), F32),
        S((tiles, 56, chans), F32), S((56, chans), F32),
        S((n, hid, chans), BF16), S((cells, chans), F32), S((n, cells, chans), BF16),
        S((n, cells, chans), BF16), S((n, cells, chans), BF16),
        S((cells, hid), BF16), S((cells, hid), F32), S((cells, hid), BF16),
        S((cells, 1), F32), S((cells, 1), F32), S((cells, chans), F32),
        S((cells, chans), F32), S((cells, chans), F32),
        S((n, cells, chans), BF16), S((n, cells, chans), BF16),
        S((n, cells, chans), BF16), S((n, cells, chans), BF16),
        S((8, cells), F32), S((n, 8, cells), F32),
        S((n * hid, chans), F32), S((width, hid), F32),
        S((width, hid), BF16), S((tiles, ri, hid), BF16),
        S((n * hid, chans), BF16), S((tiles, ro, chans), BF16),
    ]
    for count in (cells // 256 * (n - 1),) + (n,) * 4 + (tiles,) * 5 + (tiles + 1,) * 2:
        scratch += [pltpu.SemaphoreType.DMA((count,)), pltpu.SemaphoreType.DMA((count,))]
    return pl.pallas_call(
        functools.partial(mega_kernel, n, tiles, factor, 256),
        out_shape=[
            jax.ShapeDtypeStruct((cells, chans), F32),
            jax.ShapeDtypeStruct((cols, rows, chans), F32),
            jax.ShapeDtypeStruct((56, chans), F32),
            jax.ShapeDtypeStruct((tiles, ri, hid), BF16),
            jax.ShapeDtypeStruct((tiles, ro, chans), BF16),
        ],
        in_specs=[SMEM_SPEC] + [VMEM_SPEC] * 7,
        out_specs=[VMEM_SPEC] * 5,
        scratch_shapes=scratch,
        compiler_params=pltpu.CompilerParams(
            collective_id=1, has_side_effects=True, vmem_limit_bytes=LIMIT
        ),
    )(partner, x, sg, taps, win, wout, gain, shift)


def body(
    field_in, sea_mask, fold_partner, kernel, ln_gain, ln_shift, w_in, w_out, layer_scale, grad_out
):
    chans, cols, rows = field_in.shape
    tiles = lax.axis_size("lon")
    n = lax.axis_size("ch")
    cells = cols * rows
    hid = w_in.shape[1]
    factor = 1.0 / math.sqrt(tiles * cells)

    ocean_f = sea_mask.astype(F32)[None]
    masked = (field_in * sea_mask.astype(BF16)[None]).transpose(1, 2, 0)
    grad_f = grad_out.astype(F32)
    scaled_grad = (
        (ocean_f * layer_scale[:, None, None] * grad_f)
        .astype(BF16)
        .transpose(1, 2, 0)
        .reshape(cells, chans)
    )
    taps = jnp.pad(kernel.reshape(chans, 49).T, ((0, 7), (0, 0)))
    branch, field_grad, kernel_total, gw_in, gw_out = mega(
        fold_partner,
        masked,
        scaled_grad,
        taps,
        w_in.reshape(n, chans, hid),
        w_out,
        ln_gain.reshape(n, 1, chans),
        ln_shift.reshape(n, 1, chans),
        factor,
    )
    block_out = (
        ocean_f
        * (
            field_in.astype(F32)
            + layer_scale[:, None, None] * branch.T.reshape(chans, cols, rows)
        )
    ).astype(BF16)
    grad_x = (ocean_f * (grad_f + field_grad.transpose(2, 0, 1))).astype(BF16)
    kernel_grad = kernel_total[:49].T.reshape(chans, 7, 7) * factor
    gw_in = gw_in.reshape(n * chans, hid).astype(F32)
    gw_out = gw_out.reshape(n, hid, chans).transpose(1, 0, 2).reshape(hid, n * chans).astype(F32)
    return (block_out, grad_x, kernel_grad, gw_in, gw_out)


def solution(mesh):
    placed = (
        P("ch", ("grp", "lon"), None),
        P("lon", None),
        P(),
        P("ch", None, None),
        P(),
        P(),
        P(None, "ch"),
        P("ch", None),
        P("ch"),
        P("ch", ("grp", "lon"), None),
    )
    return jax.shard_map(
        body,
        mesh=mesh,
        in_specs=placed,
        out_specs=(
            P("ch", ("grp", "lon"), None),
            P("ch", ("grp", "lon"), None),
            P(("grp", "ch"), None, None),
            P("grp", "ch"),
            P(("grp", "ch"), None),
        ),
        check_vma=False,
    )
```

```python
import functools
import math

import jax
import jax.numpy as jnp
from jax import lax
from jax.experimental import pallas as pl
from jax.experimental.pallas import tpu as pltpu
from jax.sharding import PartitionSpec as P

EPSILON = 1e-06
F32 = jnp.float32
BF16 = jnp.bfloat16
MESH = pl.DeviceIdType.MESH
VMEM_SPEC = pl.BlockSpec(memory_space=pltpu.VMEM)
SMEM_SPEC = pl.BlockSpec(memory_space=pltpu.SMEM)
LIMIT = 48 * 1024 * 1024


def greet(axes):
    barrier = pltpu.get_barrier_semaphore()
    total = 0
    for axis in axes:
        count = lax.axis_size(axis)
        me = lax.axis_index(axis)
        for d in range(1, count):
            pl.semaphore_signal(
                barrier, inc=1, device_id={axis: lax.rem(me + d, count)}, device_id_type=MESH
            )
        total += count - 1
    pl.semaphore_wait(barrier, total)


def push(src, dst, sems, slot, axis, target):
    copy = pltpu.make_async_remote_copy(
        src_ref=src,
        dst_ref=dst,
        send_sem=sems[0].at[slot],
        recv_sem=sems[1].at[slot],
        device_id={axis: target},
        device_id_type=MESH,
    )
    copy.start()
    return copy


def gelu_parts(hidden):
    normal_cdf = 0.5 * (1.0 + lax.erf(hidden * (1.0 / math.sqrt(2.0))))
    density = jnp.exp(-0.5 * hidden * hidden) * (1.0 / math.sqrt(2.0 * math.pi))
    return (hidden * normal_cdf, normal_cdf + hidden * density)


def dot(a, b, dims):
    return lax.dot_general(a, b, (dims, ((), ())), preferred_element_type=F32)


def fill_shifts(ext_ref, shifts_ref, rows):
    def one(q, _):
        for b in range(7):
            shifts_ref[b, q] = ext_ref[q, pl.ds(5 + b, rows)]
        return 0

    lax.fori_loop(0, ext_ref.shape[0], one, 0)


def send_edges(x_ref, pack, west, east, tops, sems, me, tiles):
    cols, rows, chans = x_ref.shape
    right, left = lax.rem(me + 1, tiles), lax.rem(me + tiles - 1, tiles)
    copies = [
        push(x_ref.at[pl.ds(cols - 3, 3)], west, sems, 0, "lon", right),
        push(x_ref.at[pl.ds(0, 3)], east, sems, tiles, "lon", left),
    ]
    for col in range(cols):
        top = x_ref[col, pl.ds(rows - 16, 16)].astype(F32)
        for k in range(3):
            pack[pl.ds(col * 3 + k, 1)] = top[15 - k : 16 - k]
    tops[me] = pack[...].astype(BF16)
    for d in range(1, tiles):
        t = lax.rem(me + d, tiles)
        copies.append(push(tops.at[me], tops.at[me], sems, d, "lon", t))
    return copies


def mega_kernel(n, tiles, factor, block,
                partner_ref, x_ref, sg_ref, tap_ref, win_ref, wout_all, gain_ref, shift_ref,
                branch_ref, fg_ref, kernel_ref, agi, ago,
                ext_ref, shifts_ref, fold_ref, pack, west, east, tops, west2, east2, tops2,
                half_ref, sums_ref, extras_ref, extra_ref, wout_ref, mix_ref, sgg,
                mixg, normed, act, agrad, hg, mean, inv, own_ng, one_acc, two_acc,
                nsend, nrecv, bsend, brecv, psend, precv,
                gof, gif, gsi, gri, gso, gro,
                *sem_refs):
    cols, rows, chans = x_ref.shape
    cells = cols * rows
    hid = win_ref.shape[2]
    width = n * chans
    blocks = cells // block
    (m_sems, n_sems, p_sems, b_sems, s_sems, i_sems, o_sems, ai_sems, ao_sems, k_sems,
     e_sems, f_sems) = [(sem_refs[2 * k], sem_refs[2 * k + 1]) for k in range(12)]
    me = lax.axis_index("ch")
    lon = lax.axis_index("lon")
    greet(("ch", "lon"))
    chips = n // 2
    chip, core = me // 2, lax.rem(me, 2)
    peers = [
        lax.rem(chip + d // 2, chips) * 2 + lax.rem(core + d % 2, 2) for d in range(n)
    ]
    far_first = list(range(2, n)) + [1]
    spans = [lax.rem(lon + d, tiles) for d in range(tiles)]

    def loop(step):
        def one(i, _):
            step(pl.ds(pl.multiple_of(i * block, block), block))
            return 0

        lax.fori_loop(0, blocks, one, 0)

    pack[...] = jnp.zeros_like(pack)
    ecopies = send_edges(x_ref, pack, west, east, tops, e_sems, lon, tiles)
    sfar = [push(sg_ref, sgg.at[me], s_sems, c, "ch", peers[2 * c]) for c in range(1, chips)]
    scopies = [push(sg_ref, sgg.at[me], s_sems, 0, "ch", peers[1])]
    sgg[me] = sg_ref[...]
    for j in range(n):
        wout_ref[j] = wout_all[:, j * chans : (j + 1) * chans]
    ext_ref[...] = jnp.zeros_like(ext_ref)
    fold_ref[...] = jnp.zeros_like(fold_ref)
    for q in range(cols):
        ext_ref[q + 3, pl.ds(8, rows)] = x_ref[q].astype(F32)
    for copy in ecopies:
        copy.wait()
    for c in range(1, chips):
        sfar[c - 1].wait()
        view = sgg.at[lax.rem(chip - c + chips, chips) * 2 + core]
        scopies.append(push(view, view, s_sems, chips - 1 + c, "ch", peers[1]))

    for q in range(3):
        ext_ref[q, pl.ds(8, rows)] = west[q].astype(F32)
        ext_ref[cols + 3 + q, pl.ds(8, rows)] = east[q].astype(F32)
    for step in (-1, 0, 1):
        tile = lax.rem(lon + step + tiles, tiles)
        top = tops[partner_ref[tile]].astype(F32)
        for q in range(cols + 6):
            if (q - 3) // cols == step:
                base = (cols - 1 - (q - 3) % cols) * 3
                ext_ref[q, pl.ds(8 + rows, 3)] = top[base : base + 3]
    fill_shifts(ext_ref, shifts_ref, rows)

    def conv(i, _):
        acc = jnp.zeros((rows, chans), F32)
        for a in range(7):
            for b in range(7):
                acc = acc + tap_ref[pl.ds(a * 7 + b, 1)] * shifts_ref[b, i + a]
        cut = pl.ds(pl.multiple_of(i * rows, rows), rows)
        mix_ref[cut] = acc
        mixg[me, cut] = acc.astype(BF16)
        return 0

    def push_block(owner, k, slot, target):
        view = mixg.at[owner, pl.ds(k * block, block)]
        return push(view, view, m_sems, slot * blocks + k, "ch", target)

    near, far = [], []
    per = cols // blocks
    for k in range(blocks):
        lax.fori_loop(k * per, (k + 1) * per, conv, 0)
        far.append([push_block(me, k, c, peers[2 * c]) for c in range(1, chips)])
        near.append([push_block(me, k, 0, peers[1])])
    for copy in scopies:
        copy.wait()

    def grads(cut):
        total = dot(sgg[0, cut], wout_ref[0], ((1,), (1,)))
        for j in range(1, n):
            total = total + dot(sgg[j, cut], wout_ref[j], ((1,), (1,)))
        agrad[cut] = total

    loop(grads)

    def forward(cut):
        parts = [mixg[j, cut].astype(F32) for j in range(n)]
        one = functools.reduce(jnp.add, parts)
        two = functools.reduce(jnp.add, [v * v for v in parts])
        mean_cell = jnp.sum(one, axis=1, keepdims=True) / width
        sigma = lax.rsqrt(
            jnp.sum(two, axis=1, keepdims=True) / width - mean_cell * mean_cell + EPSILON
        )
        mean[cut] = mean_cell
        inv[cut] = sigma
        hidden = jnp.zeros((block, hid), F32)
        for j in range(n):
            value = ((parts[j] - mean_cell) * sigma * gain_ref[j] + shift_ref[j]).astype(BF16)
            normed[j, cut] = value
            hidden = hidden + dot(value, win_ref[j], ((1,), (0,)))
        activation, slope = gelu_parts(hidden)
        act[cut] = activation.astype(BF16)
        hg[cut] = (agrad[cut] * slope).astype(BF16)
        one_acc[cut] = jnp.zeros((block, chans), F32)
        two_acc[cut] = jnp.zeros((block, chans), F32)

    for k in range(blocks):
        for c in range(1, chips):
            far[k][c - 1].wait()
            owner = lax.rem(chip - c + chips, chips) * 2 + core
            near[k].append(push_block(owner, k, chips - 1 + c, peers[1]))
        for copy in near[k]:
            copy.wait()
        forward(pl.ds(k * block, block))

    ro, ri = n * hid // tiles, width // tiles
    for j in range(n):
        part = dot(act[...], sgg[j], ((0,), (0,)))
        gof[pl.ds(j * hid, hid)] = part
        gso[pl.ds(j * hid, hid)] = part.astype(BF16)
    ocopies, icopies = [], []
    for d in range(1, tiles):
        src = gso.at[pl.ds(pl.multiple_of(spans[d] * ro, ro), ro)]
        ocopies.append(push(src, gro.at[d], o_sems, d, "lon", spans[d]))

    ncopies = []
    for d in far_first + [0]:
        t = peers[d]

        def back(cut, d=d, t=t):
            part = dot(hg[cut], win_ref[t], ((1,), (1,)))
            if d:
                nsend[d, cut] = part.astype(BF16)
            else:
                own_ng[cut] = part
            scaled = part * gain_ref[t]
            centred = (mixg[t, cut].astype(F32) - mean[cut]) * inv[cut]
            one_acc[cut] += scaled
            two_acc[cut] += scaled * centred

        loop(back)
        if d:
            ncopies.append(push(nsend.at[d], nrecv.at[d], n_sems, d, "ch", t))
    lane = lax.broadcasted_iota(jnp.int32, (cells, 128), 1)
    pair = jnp.where(
        lane == 0,
        jnp.sum(one_acc[...], axis=1, keepdims=True),
        jnp.sum(two_acc[...], axis=1, keepdims=True),
    )
    psend[...] = pair.T[:8]
    pcopies = [push(psend, precv.at[d], p_sems, d, "ch", peers[d]) for d in range(1, n)]

    for j in range(n):
        part = dot(normed[j], hg[...], ((0,), (0,)))
        gif[pl.ds(j * chans, chans)] = part
        gsi[pl.ds(j * chans, chans)] = part.astype(BF16)
    for d in range(1, tiles):
        src = gsi.at[pl.ds(pl.multiple_of(spans[d] * ri, ri), ri)]
        icopies.append(push(src, gri.at[d], i_sems, d, "lon", spans[d]))

    bcopies = []
    for d in far_first:
        t = peers[d]

        def out(cut, d=d, t=t):
            bsend[d, cut] = dot(act[cut], wout_ref[t], ((1,), (0,))).astype(BF16)

        loop(out)
        bcopies.append(push(bsend.at[d], brecv.at[d], b_sems, d, "ch", t))

    def out_own(cut):
        branch_ref[cut] = dot(act[cut], wout_ref[me], ((1,), (0,)))

    loop(out_own)

    for copy in pcopies + ncopies:
        copy.wait()
    sums = psend[...]
    for d in range(1, n):
        sums = sums + precv[d]
    both = jnp.concatenate([sums, jnp.zeros((120, cells), F32)], axis=0).T
    one_mean = both[:, 0:1] / width
    two_mean = both[:, 1:2] / width
    total = own_ng[...]
    for d in range(1, n):
        total = total + nrecv[d].astype(F32)
    centred = (mix_ref[...] - mean[...]) * inv[...]
    own_ng[...] = inv[...] * (total * gain_ref[me] - one_mean - centred * two_mean)
    half_ref[...] = own_ng[...].astype(BF16).reshape(cols, rows, chans)
    fcopies = send_edges(half_ref, pack, west2, east2, tops2, f_sems, lon, tiles)

    acopies = []
    for copies, own, recv, held, size, sems in (
        (ocopies, gof, gro, ago, ro, ao_sems),
        (icopies, gif, gri, agi, ri, ai_sems),
    ):
        for copy in copies:
            copy.wait()
        total = own[pl.ds(pl.multiple_of(lon * size, size), size)]
        for d in range(1, tiles):
            total = total + recv[d].astype(F32)
        held[lon] = (total * factor).astype(BF16)
        for d in range(1, tiles):
            acopies.append(push(held.at[lon], held.at[lon], sems, d, "lon", spans[d]))

    sums_ref[...] = jnp.zeros_like(sums_ref)
    extra_ref[...] = jnp.zeros_like(extra_ref)

    def tap_grad(i, _):
        mg = own_ng[pl.ds(pl.multiple_of(i * rows, rows), rows)]
        for a in range(7):
            for b in range(7):
                prod = shifts_ref[b, i + a] * mg
                sums_ref[a * 7 + b] += jnp.sum(prod.reshape(rows // 8, 8, chans), axis=0)
        return 0

    lax.fori_loop(0, cols, tap_grad, 0)
    for t in range(49):
        extra_ref[pl.ds(t, 1)] = jnp.sum(sums_ref[t], axis=0, keepdims=True)
    kcopies = [
        push(extra_ref, extras_ref.at[lon], k_sems, d, "lon", spans[d])
        for d in range(1, tiles)
    ]
    extras_ref[lon] = extra_ref[...]

    for q in range(cols):
        ext_ref[q + 3, pl.ds(8, rows)] = own_ng[pl.ds(q * rows, rows)]
    for q in range(cols + 6):
        ext_ref[q, pl.ds(8 + rows, 8)] = jnp.zeros((8, chans), F32)
    for copy in fcopies:
        copy.wait()
    for q in range(3):
        ext_ref[q, pl.ds(8, rows)] = west2[q].astype(F32)
        ext_ref[cols + 3 + q, pl.ds(8, rows)] = east2[q].astype(F32)
    for step in (-1, 0, 1):
        tile = lax.rem(partner_ref[lon] + step + tiles, tiles)
        top = tops2[tile].astype(F32)
        for q in range(cols + 6):
            if (q - 3) // cols == step:
                base = (q - 3) % cols * 3
                for s in range(3):
                    fold_ref[s, q, pl.ds(5 + s, 3 - s)] = top[base : base + 3 - s]
    fill_shifts(ext_ref, shifts_ref, rows)

    def spread(i, _):
        acc = jnp.zeros((rows, chans), F32)
        for a in range(7):
            for b in range(7):
                acc = acc + tap_ref[pl.ds(a * 7 + b, 1)] * shifts_ref[6 - b, i + 6 - a]
        fg_ref[i] = acc
        north = jnp.zeros((8, chans), F32)
        for a in range(7):
            for s in range(3):
                north = north + tap_ref[pl.ds(a * 7 + 6 - s, 1)] * fold_ref[
                    s, cols - 1 - i + 6 - a
                ]
        fg_ref[i, pl.ds(rows - 8, 8)] += north
        return 0

    lax.fori_loop(0, cols, spread, 0)

    for copy in bcopies:
        copy.wait()
    total = branch_ref[...]
    for d in range(1, n):
        total = total + brecv[d].astype(F32)
    branch_ref[...] = total
    for copy in kcopies:
        copy.wait()
    kernel_ref[...] = jnp.sum(extras_ref[...], axis=0)
    for copy in acopies:
        copy.wait()


def mega(partner, x, sg, taps, win, wout, gain, shift, factor):
    cols, rows, chans = x.shape
    cells = cols * rows
    n, _, hid = win.shape
    tiles = lax.axis_size("lon")
    width = n * chans
    ro, ri = n * hid // tiles, width // tiles
    top_rows = -(-cols * 3 // 16) * 16
    S = pltpu.VMEM
    scratch = [
        S((cols + 6, rows + 16, chans), F32), S((7, cols + 6, rows, chans), F32),
        S((3, cols + 6, 8, chans), F32), S((top_rows, chans), F32),
        S((3, rows, chans), BF16), S((3, rows, chans), BF16), S((tiles, top_rows, chans), BF16),
        S((3, rows, chans), BF16), S((3, rows, chans), BF16), S((tiles, top_rows, chans), BF16),
        S((cols, rows, chans), BF16), S((49, 8, chans), F32),
        S((tiles, 56, chans), F32), S((56, chans), F32),
        S((n, hid, chans), BF16), S((cells, chans), F32), S((n, cells, chans), BF16),
        S((n, cells, chans), BF16), S((n, cells, chans), BF16),
        S((cells, hid), BF16), S((cells, hid), F32), S((cells, hid), BF16),
        S((cells, 1), F32), S((cells, 1), F32), S((cells, chans), F32),
        S((cells, chans), F32), S((cells, chans), F32),
        S((n, cells, chans), BF16), S((n, cells, chans), BF16),
        S((n, cells, chans), BF16), S((n, cells, chans), BF16),
        S((8, cells), F32), S((n, 8, cells), F32),
        S((n * hid, chans), F32), S((width, hid), F32),
        S((width, hid), BF16), S((tiles, ri, hid), BF16),
        S((n * hid, chans), BF16), S((tiles, ro, chans), BF16),
    ]
    for count in (cells // 256 * (n - 1),) + (n,) * 4 + (tiles,) * 5 + (tiles + 1,) * 2:
        scratch += [pltpu.SemaphoreType.DMA((count,)), pltpu.SemaphoreType.DMA((count,))]
    return pl.pallas_call(
        functools.partial(mega_kernel, n, tiles, factor, 256),
        out_shape=[
            jax.ShapeDtypeStruct((cells, chans), F32),
            jax.ShapeDtypeStruct((cols, rows, chans), F32),
            jax.ShapeDtypeStruct((56, chans), F32),
            jax.ShapeDtypeStruct((tiles, ri, hid), BF16),
            jax.ShapeDtypeStruct((tiles, ro, chans), BF16),
        ],
        in_specs=[SMEM_SPEC] + [VMEM_SPEC] * 7,
        out_specs=[VMEM_SPEC] * 5,
        scratch_shapes=scratch,
        compiler_params=pltpu.CompilerParams(
            collective_id=1, has_side_effects=True, vmem_limit_bytes=LIMIT
        ),
    )(partner, x, sg, taps, win, wout, gain, shift)


def body(
    field_in, sea_mask, fold_partner, kernel, ln_gain, ln_shift, w_in, w_out, layer_scale, grad_out
):
    chans, cols, rows = field_in.shape
    tiles = lax.axis_size("lon")
    n = lax.axis_size("ch")
    cells = cols * rows
    hid = w_in.shape[1]
    factor = 1.0 / math.sqrt(tiles * cells)

    ocean_f = sea_mask.astype(F32)[None]
    masked = (field_in * sea_mask.astype(BF16)[None]).transpose(1, 2, 0)
    grad_f = grad_out.astype(F32)
    scaled_grad = (
        (ocean_f * layer_scale[:, None, None] * grad_f)
        .astype(BF16)
        .transpose(1, 2, 0)
        .reshape(cells, chans)
    )
    taps = jnp.pad(kernel.reshape(chans, 49).T, ((0, 7), (0, 0)))
    branch, field_grad, kernel_total, gw_in, gw_out = mega(
        fold_partner,
        masked,
        scaled_grad,
        taps,
        w_in.reshape(n, chans, hid),
        w_out,
        ln_gain.reshape(n, 1, chans),
        ln_shift.reshape(n, 1, chans),
        factor,
    )
    block_out = (
        ocean_f
        * (
            field_in.astype(F32)
            + layer_scale[:, None, None] * branch.T.reshape(chans, cols, rows)
        )
    ).astype(BF16)
    grad_x = (ocean_f * (grad_f + field_grad.transpose(2, 0, 1))).astype(BF16)
    kernel_grad = kernel_total[:49].T.reshape(chans, 7, 7) * factor
    gw_in = gw_in.reshape(n * chans, hid).astype(F32)
    gw_out = gw_out.reshape(n, hid, chans).transpose(1, 0, 2).reshape(hid, n * chans).astype(F32)
    return (block_out, grad_x, kernel_grad, gw_in, gw_out)


def solution(mesh):
    placed = (
        P("ch", ("grp", "lon"), None),
        P("lon", None),
        P(),
        P("ch", None, None),
        P(),
        P(),
        P(None, "ch"),
        P("ch", None),
        P("ch"),
        P("ch", ("grp", "lon"), None),
    )
    return jax.shard_map(
        body,
        mesh=mesh,
        in_specs=placed,
        out_specs=(
            P("ch", ("grp", "lon"), None),
            P("ch", ("grp", "lon"), None),
            P(("grp", "ch"), None, None),
            P("grp", "ch"),
            P(("grp", "ch"), None),
        ),
        check_vma=False,
    )
```
